128 devices in a mesh: up: 8 (over x_lo, y), dn: 16 (over x_hi, z, core).
Axes of the slice: x: 4 (x_hi: 2, x_lo: 2; x = x_hi * 2 + x_lo), y: 4, z: 4, core: 2. Of those that a mesh axis runs over, the one named last changes fastest.
Arguments:
- coefficients: float32 [16384, 8192], P('up', 'dn'), may hold values from -6 to 6
- hopping_up: float32 [8, 128, 128], replicated, may hold values from -0.375 to 0.375
- partner_bits_up: int32 [7], replicated, may hold values from 0 to 6, each once
- block_signs_up: int32 [7, 128], replicated, may hold values from -2 to 2
- hopping_down: float32 [7, 128, 128], replicated, may hold values from -0.375 to 0.375
- partner_bits_down: int32 [6], replicated, may hold values from 0 to 5, each once
- block_signs_down: int32 [6, 64], replicated, may hold values from -2 to 2
- occupied_up: int32 [14, 16384], P(None, 'up'), may hold values 0 or 1
- occupied_down: int32 [14, 8192], P(None, 'dn'), may hold values 0 or 1
- site_energy: float32 [14], replicated, may hold values from 0.1 to 0.5
- repulsion: float32 [14], replicated, may hold values from 0.25 to 1
- energy_shift: float32 [], replicated, may hold values from -3 to -1
Outputs:
- residual: float32 [16384, 8192], P('up', 'dn')
- updated: float32 [16384, 8192], P('up', 'dn')
The draws below stay inside these ranges and needn't reach their ends.
Inputs may be any that keep to these rules, and one draw needn't show every extreme that they name: `partner_bits_up`: each bit number of an up block appears exactly once. `partner_bits_down`: each bit number of a down block appears exactly once.
All inputs are finite; a program needn't handle non-finite values. No bound on the sum of `occupied_up` or of `occupied_down` on one device may be relied on, other than what follows from the above.
Results may differ from the reference program's by a relative error of at most 0.0001.
Values sent between devices are 32-bit elements; how exact they have to be, the bound alone decides.
No kernel may reach another device: no remote copies, remote signals or barrier semaphores. Data moves between devices by JAX's collectives and lax.ppermute only.
A program may use at most 192 MiB of HBM per device.

```python
import math
import jax
import jax.numpy as jnp
from jax import lax

BLK = 128
ABITS = 7
DBITS = 6
SITES = 14
NA = 16384
NB = 8192


def touch_ends(entries, key, smallest, top_value):
    index_at = [jax.random.randint(jax.random.fold_in(key, axis), (), 0, length) for axis, length in enumerate(entries.shape)]
    widest = entries.shape.index(max(entries.shape))
    neighbour = index_at[:widest] + [(index_at[widest] + 1) % entries.shape[widest]] + index_at[widest + 1:]
    return entries.at[tuple(index_at)].set(smallest).at[tuple(neighbour)].set(top_value)


def level_of(rng, extent, shards, low, high):
    level, own = 1.0, jax.random.fold_in(rng, 6)
    for position, blocks in shards:
        heights = jnp.exp(jax.random.uniform(jax.random.fold_in(own, position), (blocks,), jnp.float32, low / len(shards), high / len(shards)))
        level = level * jnp.repeat(heights, extent[position] // blocks).reshape([-1 if axis == position else 1 for axis in range(len(extent))])
    return level


def bell_draw(rng, shape, spread, most, split=(), held_as=jnp.bfloat16):
    gain = level_of(rng, shape, split, -0.22, 0.18) if split else 1.0
    values = jax.random.normal(rng, shape, jnp.float32) * spread * gain
    return jnp.minimum(jnp.maximum(values, -most), most).astype(held_as)


def setup_inputs(seed: int = 0) -> dict:
    streams_of = jax.random.split(jax.random.key(seed), 13)
    coefficients = bell_draw(streams_of[0], (NA, NB), 1.0, 6.0, ((0, 8), (1, 16)), jnp.float32)
    hopping_up = bell_draw(streams_of[1], (ABITS + 1, BLK, BLK), (2 * BLK) ** -0.5, 0.375, (), jnp.float32)
    partner_bits_up = jax.random.permutation(streams_of[2], ABITS).astype(jnp.int32)
    block_signs_up = touch_ends(jax.random.randint(streams_of[3], (ABITS, NA // BLK), -2, 3), jax.random.fold_in(streams_of[3], 1), -2, 2).astype(jnp.int32)
    hopping_down = bell_draw(streams_of[4], (DBITS + 1, BLK, BLK), (2 * BLK) ** -0.5, 0.375, (), jnp.float32)
    partner_bits_down = jax.random.permutation(streams_of[5], DBITS).astype(jnp.int32)
    block_signs_down = touch_ends(jax.random.randint(streams_of[6], (DBITS, NB // BLK), -2, 3), jax.random.fold_in(streams_of[6], 1), -2, 2).astype(jnp.int32)
    occupied_up = touch_ends((jax.random.randint(streams_of[7], (SITES, NA), 0, 2) < 1).astype(jnp.int32), jax.random.fold_in(streams_of[7], 1), 0, 1)
    occupied_down = touch_ends((jax.random.randint(streams_of[8], (SITES, NB), 0, 2) < 1).astype(jnp.int32), jax.random.fold_in(streams_of[8], 1), 0, 1)
    site_energy = jnp.clip(jnp.exp(jax.random.uniform(streams_of[9], (SITES,), jnp.float32, math.log(0.1), math.log(0.5))), 0.1, 0.5)
    repulsion = jnp.clip(jnp.exp(jax.random.uniform(streams_of[10], (SITES,), jnp.float32, math.log(0.25), math.log(1.0))), 0.25, 1.0)
    energy_shift = jnp.clip(jax.random.uniform(streams_of[11], (), jnp.float32, -3.0, -1.0), -3.0, -1.0)
    return {"coefficients": coefficients, "hopping_up": hopping_up, "partner_bits_up": partner_bits_up, "block_signs_up": block_signs_up, "hopping_down": hopping_down, "partner_bits_down": partner_bits_down, "block_signs_down": block_signs_down, "occupied_up": occupied_up, "occupied_down": occupied_down, "site_energy": site_energy, "repulsion": repulsion, "energy_shift": energy_shift}


def hop_blocks(blocks, hopping, partner_bits, block_signs):
    block_count = blocks.shape[0]
    result = jnp.einsum("ij,pjw->piw", hopping[0], blocks, precision=lax.Precision.HIGHEST)
    numbers = jnp.arange(block_count, dtype=jnp.int32)
    for term_index in range(hopping.shape[0] - 1):
        flipper = jnp.left_shift(jnp.int32(1), partner_bits[term_index].astype(jnp.int32)).astype(jnp.int32)
        partner = jnp.bitwise_xor(numbers, flipper).astype(jnp.int32)
        moved = blocks[partner]
        product = jnp.einsum("ij,pjw->piw", hopping[term_index + 1], moved, precision=lax.Precision.HIGHEST)
        result = result + block_signs[term_index].astype(jnp.float32)[:, None, None] * product
    return result


def reference(coefficients, hopping_up, partner_bits_up, block_signs_up, hopping_down, partner_bits_down, block_signs_down, occupied_up, occupied_down, site_energy, repulsion, energy_shift):
    row_count, col_count = coefficients.shape
    up_blocks = coefficients.reshape(row_count // BLK, BLK, col_count)
    up_term = hop_blocks(up_blocks, hopping_up, partner_bits_up, block_signs_up).reshape(row_count, col_count)
    down_blocks = coefficients.T.reshape(col_count // BLK, BLK, row_count)
    down_term = hop_blocks(down_blocks, hopping_down, partner_bits_down, block_signs_down).reshape(col_count, row_count).T
    occ_up_f = occupied_up.astype(jnp.float32)
    occ_down_f = occupied_down.astype(jnp.float32)
    energy_up = jnp.dot(site_energy, occ_up_f, precision=lax.Precision.HIGHEST)
    energy_down = jnp.dot(site_energy, occ_down_f, precision=lax.Precision.HIGHEST)
    scaled_up = repulsion[:, None] * occ_up_f
    interaction = jnp.dot(scaled_up.T, occ_down_f, precision=lax.Precision.HIGHEST)
    diagonal = energy_up[:, None] + energy_down[None, :] + interaction
    sigma = up_term + down_term + diagonal * coefficients
    residual = sigma - energy_shift * coefficients
    updated = coefficients - residual / (diagonal - energy_shift)
    return residual, updated
```

```python
import functools

import jax
import jax.numpy as jnp
from jax import lax
from jax.experimental import pallas as pl
from jax.experimental.pallas import tpu as pltpu
from jax.sharding import PartitionSpec as P

BLK = 128
CHUNKS = 4
WINDOW = 4
STEP = 256
MASKS = {
    "A": {"x": (4, 0), "y": (1, 0), "z": (0, 2)},
    "B": {"x": (4, 8), "y": (3, 0), "z": (0, 6)},
}
TURN = ("xyz", "yzx")
SMEM = pl.BlockSpec(memory_space=pltpu.SMEM)
F32 = jnp.float32
B16 = jnp.bfloat16


def whole(shape):
    return pl.BlockSpec(shape, lambda *_: (0,) * len(shape))


def params(mib):
    return pltpu.CompilerParams(vmem_limit_bytes=mib << 20)


def exchange(x, mask0, mask1):
    ups, dns = lax.axis_size("up"), lax.axis_size("dn")
    pairs = []
    for u in range(ups):
        for d in range(dns):
            mu, md = (mask0, mask1)[d % 2]
            pairs.append((u * dns + d, (u ^ mu) * dns + (d ^ md)))
    return lax.ppermute(x, ("up", "dn"), pairs)


def after(x, *others):
    return lax.optimization_barrier((x,) + others)[0]


def halves(x):
    hi = x.astype(B16)
    return hi, (x - hi.astype(F32)).astype(B16)


def thirds(x):
    hi = x.astype(B16).astype(F32)
    mid = (x - hi).astype(B16).astype(F32)
    return hi, mid, (x - hi - mid).astype(B16).astype(F32)


def dot(a, b):
    return jnp.dot(a, b, preferred_element_type=F32)


def prepare(inv_up, inv_dn, sign_dn, dn_order, hop_up, hop_dn, occ_up, occ_dn, site, rep,
            up_w, loc_w, rem_w, left, right):
    for slot in range(8):
        h = hop_up[0] if slot == 0 else hop_up[1 + inv_up[slot - 1]]
        hi, lo = halves(h)
        up_w[slot, :BLK, :] = hi
        up_w[slot, BLK:, :] = lo
    loc_w[...] = jnp.zeros_like(loc_w)
    hi, lo = halves(hop_dn[0].T)
    for q in range(4):
        loc_w[q * BLK:(q + 1) * BLK, q * BLK:(q + 1) * BLK] = hi
        loc_w[q * BLK:(q + 1) * BLK, 512 + q * BLK:512 + (q + 1) * BLK] = lo
    for bit in range(2):
        h = hop_dn[1 + inv_dn[bit]].T
        for q in range(4):
            hi, lo = halves(h)
            s = sign_dn[bit, q]
            k = q ^ (1 << bit)
            hi = (hi.astype(F32) * s).astype(B16)
            lo = (lo.astype(F32) * s).astype(B16)
            loc_w[k * BLK:(k + 1) * BLK, q * BLK:(q + 1) * BLK] = hi
            loc_w[k * BLK:(k + 1) * BLK, 512 + q * BLK:512 + (q + 1) * BLK] = lo
    for t in range(4):
        bit = dn_order[t]
        h = hop_dn[1 + inv_dn[bit]].T
        for q in range(4):
            hi, lo = halves(h)
            s = sign_dn[bit, q]
            rem_w[q, t * BLK:(t + 1) * BLK, :BLK] = (hi.astype(F32) * s).astype(B16)
            rem_w[q, t * BLK:(t + 1) * BLK, BLK:] = (lo.astype(F32) * s).astype(B16)
    ou, od = occ_up[...], occ_dn[...]
    sites = thirds(site[...])
    reps = thirds(rep[...])
    for n in range(3):
        left[16 * n:16 * n + 16, :] = (reps[n] * ou).astype(B16)
        right[16 * n:16 * n + 16, :] = od.astype(B16)
        left[48 + 16 * n:64 + 16 * n, :] = (sites[n] * ou).astype(B16)
        right[48 + 16 * n:64 + 16 * n, :] = jnp.ones_like(od).astype(B16)
        left[96 + 16 * n:112 + 16 * n, :] = jnp.ones_like(ou).astype(B16)
        right[96 + 16 * n:112 + 16 * n, :] = (sites[n] * od).astype(B16)


def signed(up_w, slot, s):
    return (up_w[slot].astype(F32) * s).astype(B16)


def local_body(sign_up, own, near, far, up_w, loc_w, out):
    i = pl.program_id(0)
    own_hi, own_lo = halves(own[...])
    near_hi, near_lo = halves(near[...])
    far_hi, far_lo = halves(far[...])
    width = loc_w.shape[0]

    def rows(x, p):
        return x[p * BLK:(p + 1) * BLK]

    across = dot(own_hi, loc_w[...])
    across = across[:, :width] + across[:, width:] + dot(own_lo, loc_w[:, :width])
    for p in range(4):
        w = [up_w[0]] + [signed(up_w, 1 + b, sign_up[b, 4 * i + p]) for b in range(4)]
        w = jnp.concatenate(w, axis=1)

        def stack(o, n, f):
            return jnp.concatenate(
                [rows(o, p), rows(o, p ^ 1), rows(o, p ^ 2), rows(n, p), rows(f, p)], axis=0
            )

        r = dot(w, stack(own_hi, near_hi, far_hi))
        r = r[:BLK] + r[BLK:] + dot(w[:BLK], stack(own_lo, near_lo, far_lo))
        out[p * BLK:(p + 1) * BLK, :] = r + rows(across, p)


def final_body(first, which, sign_up, slots, shift, a0, a1, a2, b0, b1, b2, mate, acc, own, up_w, rem_w,
               left, right, *rest):
    residual, updated = rest[-2:]
    zero = which[0] == 0
    step = pl.program_id(0)
    ups = [a0[...], jnp.where(zero, a1[...], a2[...]), jnp.where(zero, b1[...], b0[...])]
    dns = [jnp.where(zero, a2[...], a1[...]), jnp.where(zero, b0[...], b1[...]), b2[...], mate[...]]
    total = acc[...]
    up_parts = [halves(x) for x in ups]
    dn_parts = [halves(x) for x in dns]
    columns = []
    for q in range(4):
        cut = slice(q * BLK, (q + 1) * BLK)
        hi = jnp.concatenate([x[0][:, cut] for x in dn_parts], axis=1)
        lo = jnp.concatenate([x[1][:, cut] for x in dn_parts], axis=1)
        r = dot(hi, rem_w[q])
        columns.append(r[:, :BLK] + r[:, BLK:] + dot(lo, rem_w[q, :, :BLK]))
    total = total + jnp.concatenate(columns, axis=1)
    blocks = []
    for p in range(STEP // BLK):
        cut = slice(p * BLK, (p + 1) * BLK)
        block = first + step * (STEP // BLK) + p
        w = jnp.concatenate(
            [signed(up_w, slots[t], sign_up[slots[t] - 1, block]) for t in range(3)], axis=1
        )
        r = dot(w, jnp.concatenate([x[0][cut] for x in up_parts], axis=0))
        blocks.append(
            r[:BLK] + r[BLK:] + dot(w[:BLK], jnp.concatenate([x[1][cut] for x in up_parts], axis=0))
        )
    total = total + jnp.concatenate(blocks, axis=0)
    gap = lax.dot_general(left[...], right[...], (((0,), (0,)), ((), ())),
                          preferred_element_type=F32) - shift[0]
    c = own[...]
    res = total + gap * c
    residual[...] = res
    updated[...] = c - res / gap


def shards(
    coefficients,
    hopping_up,
    partner_bits_up,
    block_signs_up,
    hopping_down,
    partner_bits_down,
    block_signs_down,
    occupied_up,
    occupied_down,
    site_energy,
    repulsion,
    energy_shift,
):
    rows, width = coefficients.shape
    size = rows // CHUNKS
    up_local, dn_local = rows // BLK, width // BLK
    core = lax.axis_index("dn") % 2

    def by_bit(bits, signs, first, count):
        number = bits.shape[0]
        chosen = bits[None, :] == jnp.arange(number)[:, None]
        place = jnp.sum(jnp.where(chosen, jnp.arange(number)[None, :], 0), axis=1).astype(jnp.int32)
        part = lax.dynamic_slice_in_dim(signs, first, count, axis=1)
        return place, jnp.sum(jnp.where(chosen[:, :, None], part[None], 0), axis=1).astype(F32)

    inv_up, sign_up = by_bit(partner_bits_up, block_signs_up, lax.axis_index("up") * up_local, up_local)
    inv_dn, sign_dn = by_bit(partner_bits_down, block_signs_down, lax.axis_index("dn") * dn_local, dn_local)
    slots = jnp.where(core == 0, jnp.array([7, 5, 6], jnp.int32), jnp.array([5, 7, 6], jnp.int32))
    dn_order = jnp.where(core == 0, jnp.array([3, 5, 4, 2], jnp.int32), jnp.array([3, 4, 5, 2], jnp.int32))
    which = core.astype(jnp.int32).reshape(1)

    mate = exchange(coefficients, (0, 1), (0, 1))
    order = [("A", j, 0) for j in range(3)]
    for i in range(CHUNKS):
        for j in range(3):
            order.append(("B", j, i))
            if i + 1 < CHUNKS:
                order.append(("A", j, i + 1))
    got, done = {}, []
    for n, (kind, j, i) in enumerate(order):
        if kind == "A":
            source = coefficients if n < WINDOW else after(coefficients, done[n - WINDOW])
            source = lax.slice_in_dim(source, i * size, (i + 1) * size)
        else:
            source = got["A", j, i]
            if n >= WINDOW:
                source = after(source, done[n - WINDOW])
        got[kind, j, i] = exchange(source, MASKS[kind][TURN[0][j]], MASKS[kind][TURN[1][j]])
        done.append(got[kind, j, i])

    pad = ((0, 2), (0, 0))
    up_w, loc_w, rem_w, left, right = pl.pallas_call(
        prepare,
        out_shape=[
            jax.ShapeDtypeStruct((8, 2 * BLK, BLK), B16),
            jax.ShapeDtypeStruct((width, 2 * width), B16),
            jax.ShapeDtypeStruct((4, 4 * BLK, 2 * BLK), B16),
            jax.ShapeDtypeStruct((144, rows), B16),
            jax.ShapeDtypeStruct((144, width), B16),
        ],
        in_specs=[SMEM] * 4 + [pl.BlockSpec(memory_space=pltpu.VMEM)] * 6,
        compiler_params=params(24),
        cost_estimate=pl.CostEstimate(flops=0, bytes_accessed=8 << 20, transcendentals=0),
        name="prepare",
    )(
        inv_up, inv_dn, sign_dn, dn_order, hopping_up, hopping_down,
        jnp.pad(occupied_up.astype(F32), pad), jnp.pad(occupied_down.astype(F32), pad),
        jnp.pad(site_energy[:, None], pad), jnp.pad(repulsion[:, None], pad),
    )

    block = (size, width)
    acc = pl.pallas_call(
        local_body,
        grid=(CHUNKS,),
        out_shape=jax.ShapeDtypeStruct((rows, width), F32),
        in_specs=[
            SMEM,
            pl.BlockSpec(block, lambda i: (i, 0)),
            pl.BlockSpec(block, lambda i: (i ^ 1, 0)),
            pl.BlockSpec(block, lambda i: (i ^ 2, 0)),
            whole(up_w.shape),
            whole(loc_w.shape),
        ],
        out_specs=pl.BlockSpec(block, lambda i: (i, 0)),
        compiler_params=params(36),
        cost_estimate=pl.CostEstimate(flops=12 << 30, bytes_accessed=24 << 20, transcendentals=0),
        name="local",
    )(sign_up, coefficients, coefficients, coefficients, up_w, loc_w)

    outs = None
    tile = (STEP, width)
    steps = size // STEP
    for i in range(CHUNKS):
        base = i * steps
        here = pl.BlockSpec(tile, lambda s: (s, 0))
        there = pl.BlockSpec(tile, lambda s, base=base: (base + s, 0))
        arrived = [got[k, j, i] for k in "AB" for j in range(3)]
        extra = [] if outs is None else list(outs)
        operands = [which, sign_up, slots, energy_shift.reshape(1), *arrived, mate, acc, coefficients,
                    up_w, rem_w, left, right]
        outs = pl.pallas_call(
            functools.partial(final_body, i * (size // BLK)),
            grid=(steps,),
            out_shape=[jax.ShapeDtypeStruct((rows, width), F32)] * 2,
            in_specs=[SMEM] * 4 + [here] * 6 + [there] * 3 + [
                whole(up_w.shape),
                whole(rem_w.shape),
                pl.BlockSpec((144, STEP), lambda s, base=base: (0, base + s)),
                whole(right.shape),
            ] + [pl.BlockSpec(memory_space=pl.ANY)] * len(extra),
            out_specs=[there, there],
            input_output_aliases={len(operands): 0, len(operands) + 1: 1} if extra else {},
            compiler_params=params(36),
            cost_estimate=pl.CostEstimate(flops=3 << 30, bytes_accessed=12 << 20, transcendentals=0),
            name="finish",
        )(*operands, *extra)
    return tuple(outs)


def solution(mesh):
    placed = (
        P("up", "dn"),
        P(),
        P(),
        P(),
        P(),
        P(),
        P(),
        P(None, "up"),
        P(None, "dn"),
        P(),
        P(),
        P(),
    )
    return jax.shard_map(
        shards,
        mesh=mesh,
        in_specs=placed,
        out_specs=(P("up", "dn"), P("up", "dn")),
        check_vma=False,
    )
```

```python
import functools

import jax
import jax.numpy as jnp
from jax import lax
from jax.experimental import pallas as pl
from jax.experimental.pallas import tpu as pltpu
from jax.sharding import PartitionSpec as P

BLK = 128
SIZES = (4, 4, 5, 3)
GAP = 6
ROOM = 32
MASKS = {
    "A": {"x": (4, 0), "y": (1, 0), "z": (0, 2)},
    "B": {"x": (4, 8), "y": (3, 0), "z": (0, 6)},
}
TURN = ("xyz", "yzx")
SMEM = pl.BlockSpec(memory_space=pltpu.SMEM)
F32 = jnp.float32
B16 = jnp.bfloat16


def whole(shape):
    return pl.BlockSpec(shape, lambda *_: (0,) * len(shape))


def params(mib):
    return pltpu.CompilerParams(vmem_limit_bytes=mib << 20)


def exchange(x, mask0, mask1):
    ups, dns = lax.axis_size("up"), lax.axis_size("dn")
    pairs = []
    for u in range(ups):
        for d in range(dns):
            mu, md = (mask0, mask1)[d % 2]
            pairs.append((u * dns + d, (u ^ mu) * dns + (d ^ md)))
    return lax.ppermute(x, ("up", "dn"), pairs)


def halves(x):
    hi = x.astype(B16)
    return hi, (x - hi.astype(F32)).astype(B16)


def thirds(x):
    hi = x.astype(B16).astype(F32)
    mid = (x - hi).astype(B16).astype(F32)
    return hi, mid, (x - hi - mid).astype(B16).astype(F32)


def dot(a, b):
    return jnp.dot(a, b, preferred_element_type=F32)


def slot_of(bits, bit):
    place = jnp.int32(0)
    for k in range(bits.shape[0]):
        place = jnp.where(bits[k] == bit, k, place)
    return place


def column(values):
    row = lax.broadcasted_iota(jnp.int32, (16, BLK), 0)
    out = jnp.zeros((16, BLK), F32)
    for k in range(values.shape[0]):
        out = jnp.where(row == k, values[k], out)
    return out


def prepare(bits_up, bits_dn, signs_dn, site, rep, hop_up, hop_dn, occ_up, occ_dn,
            up_w, loc_w, rem_w, left, right, ou, od):
    dn = lax.axis_index("dn")
    count = loc_w.shape[0] // BLK
    zero = dn % 2 == 0
    for slot in range(8):
        h = hop_up[0] if slot == 0 else hop_up[1 + slot_of(bits_up, slot - 1)]
        hi, lo = halves(h)
        up_w[slot, :BLK, :] = hi
        up_w[slot, BLK:, :] = lo
    loc_w[...] = jnp.zeros_like(loc_w)
    hi, lo = halves(hop_dn[0].T)
    for q in range(4):
        loc_w[q * BLK:(q + 1) * BLK, q * BLK:(q + 1) * BLK] = hi
        loc_w[q * BLK:(q + 1) * BLK, 512 + q * BLK:512 + (q + 1) * BLK] = lo
    for bit in range(2):
        k = slot_of(bits_dn, bit)
        hi, lo = halves(hop_dn[1 + k].T)
        for q in range(4):
            s = signs_dn[k, dn * count + q].astype(F32)
            r = (q ^ (1 << bit)) * BLK
            loc_w[r:r + BLK, q * BLK:(q + 1) * BLK] = (hi.astype(F32) * s).astype(B16)
            loc_w[r:r + BLK, 512 + q * BLK:512 + (q + 1) * BLK] = (lo.astype(F32) * s).astype(B16)
    for t, bit in enumerate((3, jnp.where(zero, 5, 4), jnp.where(zero, 4, 5), 2)):
        k = slot_of(bits_dn, bit)
        hi, lo = halves(hop_dn[1 + k].T)
        for q in range(4):
            s = signs_dn[k, dn * count + q].astype(F32)
            rem_w[q, t * BLK:(t + 1) * BLK, :BLK] = (hi.astype(F32) * s).astype(B16)
            rem_w[q, t * BLK:(t + 1) * BLK, BLK:] = (lo.astype(F32) * s).astype(B16)
    sites = [x[:, :1] for x in thirds(column(site))]
    reps = [x[:, :1] for x in thirds(column(rep))]
    for raw, padded in ((occ_up, ou), (occ_dn, od)):
        padded[...] = jnp.zeros_like(padded)
        padded[:raw.shape[0], :] = raw[...].astype(F32)
    for n in range(3):
        left[16 * n:16 * n + 16, :] = (reps[n] * ou[...]).astype(B16)
        right[16 * n:16 * n + 16, :] = od[...].astype(B16)
        left[48 + 16 * n:64 + 16 * n, :] = (sites[n] * ou[...]).astype(B16)
        right[48 + 16 * n:64 + 16 * n, :] = jnp.ones_like(od).astype(B16)
        left[96 + 16 * n:112 + 16 * n, :] = jnp.ones_like(ou).astype(B16)
        right[96 + 16 * n:112 + 16 * n, :] = (sites[n] * od[...]).astype(B16)


def signed(up_w, slot, s):
    return (up_w[slot].astype(F32) * s).astype(B16)


def local_body(half, firsts, bits_up, signs_up, own, near, far, up_w, loc_w, out, *pieces):
    i = 2 * half + pl.program_id(0)
    first = lax.axis_index("up") * 16 + 4 * i
    places = [slot_of(bits_up, b) for b in range(4)]
    for k, piece in enumerate(pieces):
        low = firsts[k]
        for r in range(low, low + piece.shape[0] // BLK):
            @pl.when(i == r // 4)
            def _(r=r, low=low, piece=piece):
                piece[(r - low) * BLK:(r - low + 1) * BLK, :] = own[r % 4 * BLK:(r % 4 + 1) * BLK, :]

    own_hi, own_lo = halves(own[...])
    near_hi, near_lo = halves(near[...])
    far_hi, far_lo = halves(far[...])
    width = loc_w.shape[0]

    def rows(x, p):
        return x[p * BLK:(p + 1) * BLK]

    across = dot(own_hi, loc_w[...])
    across = across[:, :width] + across[:, width:] + dot(own_lo, loc_w[:, :width])
    for p in range(4):
        w = [up_w[0]] + [
            signed(up_w, 1 + b, signs_up[places[b], first + p].astype(F32)) for b in range(4)
        ]
        w = jnp.concatenate(w, axis=1)

        def stack(o, n, f):
            return jnp.concatenate(
                [rows(o, p), rows(o, p ^ 1), rows(o, p ^ 2), rows(n, p), rows(f, p)], axis=0
            )

        r = dot(w, stack(own_hi, near_hi, far_hi))
        r = r[:BLK] + r[BLK:] + dot(w[:BLK], stack(own_lo, near_lo, far_lo))
        out[p * BLK:(p + 1) * BLK, :] = r + rows(across, p)


def final_body(first, span, bits_up, signs_up, shift, a0, a1, a2, b0, b1, b2, mate, acc, own, up_w, rem_w,
               left, right, *rest):
    residual, updated, mark = rest[-3:]
    zero = lax.axis_index("dn") % 2 == 0
    step = pl.program_id(0)
    slots = (jnp.where(zero, 7, 5), jnp.where(zero, 5, 7), 6)
    places = [slot_of(bits_up, slot - 1) for slot in slots]
    ups = [a0[...], jnp.where(zero, a1[...], a2[...]), jnp.where(zero, b1[...], b0[...])]
    dns = [jnp.where(zero, a2[...], a1[...]), jnp.where(zero, b0[...], b1[...]), b2[...], mate[...]]
    total = acc[...]
    up_parts = [halves(x) for x in ups]
    dn_parts = [halves(x) for x in dns]
    columns = []
    for q in range(4):
        cut = slice(q * BLK, (q + 1) * BLK)
        hi = jnp.concatenate([x[0][:, cut] for x in dn_parts], axis=1)
        lo = jnp.concatenate([x[1][:, cut] for x in dn_parts], axis=1)
        r = dot(hi, rem_w[q])
        columns.append(r[:, :BLK] + r[:, BLK:] + dot(lo, rem_w[q, :, :BLK]))
    total = total + jnp.concatenate(columns, axis=1)
    blocks = []
    for p in range(span // BLK):
        cut = slice(p * BLK, (p + 1) * BLK)
        block = lax.axis_index("up") * 16 + first + step * (span // BLK) + p
        w = jnp.concatenate(
            [signed(up_w, slots[t], signs_up[places[t], block].astype(F32)) for t in range(3)], axis=1
        )
        r = dot(w, jnp.concatenate([x[0][cut] for x in up_parts], axis=0))
        blocks.append(
            r[:BLK] + r[BLK:] + dot(w[:BLK], jnp.concatenate([x[1][cut] for x in up_parts], axis=0))
        )
    total = total + jnp.concatenate(blocks, axis=0)
    gap = lax.dot_general(left[...], right[...], (((0,), (0,)), ((), ())),
                          preferred_element_type=F32) - shift[0]
    c = own[...]
    res = total + gap * c
    residual[...] = res
    updated[...] = c - res / gap
    mark[...] = res[:8, :BLK]


def shards(
    coefficients,
    hopping_up,
    partner_bits_up,
    block_signs_up,
    hopping_down,
    partner_bits_down,
    block_signs_down,
    occupied_up,
    occupied_down,
    site_energy,
    repulsion,
    energy_shift,
):
    rows, width = coefficients.shape
    chunks = len(SIZES)
    starts = [sum(SIZES[:i]) * BLK for i in range(chunks)]
    vmem = pl.BlockSpec(memory_space=pltpu.VMEM)
    up_w, loc_w, rem_w, left, right = pl.pallas_call(
        prepare,
        out_shape=[
            jax.ShapeDtypeStruct((8, 2 * BLK, BLK), B16),
            jax.ShapeDtypeStruct((width, 2 * width), B16),
            jax.ShapeDtypeStruct((4, 4 * BLK, 2 * BLK), B16),
            jax.ShapeDtypeStruct((144, rows), B16),
            jax.ShapeDtypeStruct((144, width), B16),
        ],
        in_specs=[SMEM] * 5 + [vmem] * 4,
        scratch_shapes=[pltpu.VMEM((16, rows), F32), pltpu.VMEM((16, width), F32)],
        compiler_params=params(ROOM),
        cost_estimate=pl.CostEstimate(flops=0, bytes_accessed=4 << 20, transcendentals=0),
        name="prepare",
    )(partner_bits_up, partner_bits_down, block_signs_down, site_energy, repulsion,
      hopping_up, hopping_down, occupied_up, occupied_down)

    block = (4 * BLK, width)
    parts, pieces = [], [lax.slice_in_dim(coefficients, 0, SIZES[0] * BLK)]
    for h in range(2):
        own = [i for i in range(1, chunks) if starts[i] * 2 // rows == h]
        part, *more = pl.pallas_call(
            functools.partial(local_body, h, [starts[i] // BLK for i in own]),
            grid=(2,),
            out_shape=[jax.ShapeDtypeStruct((rows // 2, width), F32)]
            + [jax.ShapeDtypeStruct((SIZES[i] * BLK, width), F32) for i in own],
            in_specs=[
                SMEM,
                SMEM,
                pl.BlockSpec(block, lambda i, h=h: (2 * h + i, 0)),
                pl.BlockSpec(block, lambda i, h=h: ((2 * h + i) ^ 1, 0)),
                pl.BlockSpec(block, lambda i, h=h: ((2 * h + i) ^ 2, 0)),
                whole(up_w.shape),
                whole(loc_w.shape),
            ],
            out_specs=[pl.BlockSpec(block, lambda i: (i, 0))] + [whole((SIZES[i] * BLK, width)) for i in own],
            compiler_params=params(ROOM),
            cost_estimate=pl.CostEstimate(flops=6 << 30, bytes_accessed=12 << 20, transcendentals=0),
            name="local",
        )(partner_bits_up, block_signs_up, coefficients, coefficients, coefficients, up_w, loc_w)
        parts.append(part)
        pieces += more

    def finish(i, outs):
        span = 2 * BLK if (SIZES[i] | starts[i] // BLK) % 2 == 0 else BLK
        tile = (span, width)
        base = starts[i] // span
        here = pl.BlockSpec(tile, lambda s: (s, 0))
        there = pl.BlockSpec(tile, lambda s: (base + s, 0))
        h = starts[i] * 2 // rows
        below = h * rows // 2 // span
        half = pl.BlockSpec(tile, lambda s: (base - below + s, 0))
        arrived = [got[k, j, i] for k in "AB" for j in range(3)]
        operands = [partner_bits_up, block_signs_up, energy_shift.reshape(1), *arrived, got["mate"], got["acc", h], coefficients,
                    up_w, rem_w, left, right]
        tail = [*outs, got["mark"]] if outs else []
        return pl.pallas_call(
            functools.partial(final_body, starts[i] // BLK, span),
            grid=(SIZES[i] * BLK // span,),
            out_shape=[jax.ShapeDtypeStruct((rows, width), F32)] * 2 + [jax.ShapeDtypeStruct((8, BLK), F32)],
            in_specs=[SMEM] * 3 + [here] * 6 + [there, half, there] + [
                whole(up_w.shape),
                whole(rem_w.shape),
                pl.BlockSpec((144, span), lambda s: (0, base + s)),
                whole(right.shape),
            ] + [pl.BlockSpec(memory_space=pl.ANY)] * len(tail),
            out_specs=[there, there, whole((8, BLK))],
            input_output_aliases={len(operands) + k: k for k in range(len(outs))},
            compiler_params=params(ROOM),
            cost_estimate=pl.CostEstimate(flops=3 << 30, bytes_accessed=12 << 20, transcendentals=0),
            name="finish",
        )(*operands, *tail)

    order = [("A", j, 0) for j in range(3)]
    for i in range(chunks):
        for j in range(3):
            order.append(("B", j, i))
            if i + 1 < chunks:
                order.append(("A", j, i + 1))
    got, outs = {}, []
    got["mate"] = exchange(coefficients, (0, 1), (0, 1))
    got["acc", 0], got["acc", 1] = parts
    for n, (kind, j, i) in enumerate(order):
        source = pieces[i] if kind == "A" else got["A", j, i]
        waits = [("acc", 0), "mate"] if n == 3 else []
        if n >= GAP and order[n - GAP][:2] == ("B", 2):
            *outs, got["mark"] = finish(order[n - GAP][2], outs)
            waits = ["mark"]
        if waits:
            source, *held = lax.optimization_barrier((source, *[got[w] for w in waits]))
            got.update(zip(waits, held))
        if kind == "B":
            got["A", j, i] = source
        got[kind, j, i] = exchange(source, MASKS[kind][TURN[0][j]], MASKS[kind][TURN[1][j]])
    for n in range(len(order), len(order) + GAP):
        if order[n - GAP][:2] == ("B", 2):
            *outs, got["mark"] = finish(order[n - GAP][2], outs)
    return tuple(outs)


def solution(mesh):
    placed = (
        P("up", "dn"),
        P(),
        P(),
        P(),
        P(),
        P(),
        P(),
        P(None, "up"),
        P(None, "dn"),
        P(),
        P(),
        P(),
    )
    return jax.shard_map(
        shards,
        mesh=mesh,
        in_specs=placed,
        out_specs=(P("up", "dn"), P("up", "dn")),
        check_vma=False,
    )
```

```python
import functools

import jax
import jax.numpy as jnp
from jax import lax
from jax.experimental import pallas as pl
from jax.experimental.pallas import tpu as pltpu
from jax.sharding import PartitionSpec as P

BLK = 128
SIZES = (4, 4, 5, 3)
GAP = 6
EARLY = (3,)
ROOM = 32
MASKS = {
    "A": {"x": (4, 0), "y": (1, 0), "z": (0, 2)},
    "B": {"x": (4, 8), "y": (3, 0), "z": (0, 6)},
}
TURN = ("xyz", "yzx")
SMEM = pl.BlockSpec(memory_space=pltpu.SMEM)
F32 = jnp.float32
B16 = jnp.bfloat16


def whole(shape):
    return pl.BlockSpec(shape, lambda *_: (0,) * len(shape))


def params(mib):
    return pltpu.CompilerParams(vmem_limit_bytes=mib << 20)


def exchange(x, mask0, mask1):
    ups, dns = lax.axis_size("up"), lax.axis_size("dn")
    pairs = []
    for u in range(ups):
        for d in range(dns):
            mu, md = (mask0, mask1)[d % 2]
            pairs.append((u * dns + d, (u ^ mu) * dns + (d ^ md)))
    return lax.ppermute(x, ("up", "dn"), pairs)


def halves(x):
    hi = x.astype(B16)
    return hi, (x - hi.astype(F32)).astype(B16)


def thirds(x):
    hi = x.astype(B16).astype(F32)
    mid = (x - hi).astype(B16).astype(F32)
    return hi, mid, (x - hi - mid).astype(B16).astype(F32)


def dot(a, b):
    return jnp.dot(a, b, preferred_element_type=F32)


def slot_of(bits, bit):
    place = jnp.int32(0)
    for k in range(bits.shape[0]):
        place = jnp.where(bits[k] == bit, k, place)
    return place


def column(values):
    row = lax.broadcasted_iota(jnp.int32, (16, BLK), 0)
    out = jnp.zeros((16, BLK), F32)
    for k in range(values.shape[0]):
        out = jnp.where(row == k, values[k], out)
    return out


def prepare(bits_up, bits_dn, signs_dn, site, rep, hop_up, hop_dn, occ_up, occ_dn,
            up_w, loc_w, rem_w, left, right, ou, od):
    dn = lax.axis_index("dn")
    count = loc_w.shape[0] // BLK
    zero = dn % 2 == 0
    for slot in range(8):
        h = hop_up[0] if slot == 0 else hop_up[1 + slot_of(bits_up, slot - 1)]
        hi, lo = halves(h)
        up_w[slot, :BLK, :] = hi
        up_w[slot, BLK:, :] = lo
    loc_w[...] = jnp.zeros_like(loc_w)
    hi, lo = halves(hop_dn[0].T)
    for q in range(4):
        loc_w[q * BLK:(q + 1) * BLK, q * BLK:(q + 1) * BLK] = hi
        loc_w[q * BLK:(q + 1) * BLK, 512 + q * BLK:512 + (q + 1) * BLK] = lo
    for bit in range(2):
        k = slot_of(bits_dn, bit)
        hi, lo = halves(hop_dn[1 + k].T)
        for q in range(4):
            s = signs_dn[k, dn * count + q].astype(F32)
            r = (q ^ (1 << bit)) * BLK
            loc_w[r:r + BLK, q * BLK:(q + 1) * BLK] = (hi.astype(F32) * s).astype(B16)
            loc_w[r:r + BLK, 512 + q * BLK:512 + (q + 1) * BLK] = (lo.astype(F32) * s).astype(B16)
    for t, bit in enumerate((3, jnp.where(zero, 5, 4), jnp.where(zero, 4, 5), 2)):
        k = slot_of(bits_dn, bit)
        hi, lo = halves(hop_dn[1 + k].T)
        for q in range(4):
            s = signs_dn[k, dn * count + q].astype(F32)
            rem_w[q, t * BLK:(t + 1) * BLK, :BLK] = (hi.astype(F32) * s).astype(B16)
            rem_w[q, t * BLK:(t + 1) * BLK, BLK:] = (lo.astype(F32) * s).astype(B16)
    sites = [x[:, :1] for x in thirds(column(site))]
    reps = [x[:, :1] for x in thirds(column(rep))]
    for raw, padded in ((occ_up, ou), (occ_dn, od)):
        padded[...] = jnp.zeros_like(padded)
        padded[:raw.shape[0], :] = raw[...].astype(F32)
    for n in range(3):
        left[16 * n:16 * n + 16, :] = (reps[n] * ou[...]).astype(B16)
        right[16 * n:16 * n + 16, :] = od[...].astype(B16)
        left[48 + 16 * n:64 + 16 * n, :] = (sites[n] * ou[...]).astype(B16)
        right[48 + 16 * n:64 + 16 * n, :] = jnp.ones_like(od).astype(B16)
        left[96 + 16 * n:112 + 16 * n, :] = jnp.ones_like(ou).astype(B16)
        right[96 + 16 * n:112 + 16 * n, :] = (sites[n] * od[...]).astype(B16)


def signed(up_w, slot, s):
    return (up_w[slot].astype(F32) * s).astype(B16)


def local_body(half, firsts, bits_up, signs_up, own, near, far, up_w, loc_w, out, *pieces):
    i = 2 * half + pl.program_id(0)
    first = lax.axis_index("up") * 16 + 4 * i
    places = [slot_of(bits_up, b) for b in range(4)]
    for k, piece in enumerate(pieces):
        low = firsts[k]
        for r in range(low, low + piece.shape[0] // BLK):
            @pl.when(i == r // 4)
            def _(r=r, low=low, piece=piece):
                piece[(r - low) * BLK:(r - low + 1) * BLK, :] = own[r % 4 * BLK:(r % 4 + 1) * BLK, :]

    own_hi, own_lo = halves(own[...])
    near_hi, near_lo = halves(near[...])
    far_hi, far_lo = halves(far[...])
    width = loc_w.shape[0]

    def rows(x, p):
        return x[p * BLK:(p + 1) * BLK]

    across = dot(own_hi, loc_w[...])
    across = across[:, :width] + across[:, width:] + dot(own_lo, loc_w[:, :width])
    for p in range(4):
        w = [up_w[0]] + [
            signed(up_w, 1 + b, signs_up[places[b], first + p].astype(F32)) for b in range(4)
        ]
        w = jnp.concatenate(w, axis=1)

        def stack(o, n, f):
            return jnp.concatenate(
                [rows(o, p), rows(o, p ^ 1), rows(o, p ^ 2), rows(n, p), rows(f, p)], axis=0
            )

        r = dot(w, stack(own_hi, near_hi, far_hi))
        r = r[:BLK] + r[BLK:] + dot(w[:BLK], stack(own_lo, near_lo, far_lo))
        out[p * BLK:(p + 1) * BLK, :] = r + rows(across, p)


def final_body(first, span, bits_up, signs_up, shift, a0, a1, a2, b0, b1, b2, mate, acc, own, up_w, rem_w,
               left, right, *rest):
    residual, updated, mark = rest[-3:]
    zero = lax.axis_index("dn") % 2 == 0
    step = pl.program_id(0)
    slots = (jnp.where(zero, 7, 5), jnp.where(zero, 5, 7), 6)
    places = [slot_of(bits_up, slot - 1) for slot in slots]
    ups = [a0[...], jnp.where(zero, a1[...], a2[...]), jnp.where(zero, b1[...], b0[...])]
    dns = [jnp.where(zero, a2[...], a1[...]), jnp.where(zero, b0[...], b1[...]), b2[...], mate[...]]
    total = acc[...]
    up_parts = [halves(x) for x in ups]
    dn_parts = [halves(x) for x in dns]
    columns = []
    for q in range(4):
        cut = slice(q * BLK, (q + 1) * BLK)
        hi = jnp.concatenate([x[0][:, cut] for x in dn_parts], axis=1)
        lo = jnp.concatenate([x[1][:, cut] for x in dn_parts], axis=1)
        r = dot(hi, rem_w[q])
        columns.append(r[:, :BLK] + r[:, BLK:] + dot(lo, rem_w[q, :, :BLK]))
    total = total + jnp.concatenate(columns, axis=1)
    blocks = []
    for p in range(span // BLK):
        cut = slice(p * BLK, (p + 1) * BLK)
        block = lax.axis_index("up") * 16 + first + step * (span // BLK) + p
        w = jnp.concatenate(
            [signed(up_w, slots[t], signs_up[places[t], block].astype(F32)) for t in range(3)], axis=1
        )
        r = dot(w, jnp.concatenate([x[0][cut] for x in up_parts], axis=0))
        blocks.append(
            r[:BLK] + r[BLK:] + dot(w[:BLK], jnp.concatenate([x[1][cut] for x in up_parts], axis=0))
        )
    total = total + jnp.concatenate(blocks, axis=0)
    gap = lax.dot_general(left[...], right[...], (((0,), (0,)), ((), ())),
                          preferred_element_type=F32) - shift[0]
    c = own[...]
    res = total + gap * c
    residual[...] = res
    updated[...] = c - res / gap
    mark[...] = res[:8, :BLK]


def remote(first, span, bits_up, signs_up, slots, ups, dns, up_w, weight):
    step = pl.program_id(0)
    places = [slot_of(bits_up, slot - 1) for slot in slots]
    up_parts = [halves(x) for x in ups]
    dn_parts = [halves(x) for x in dns]
    columns = []
    for q in range(4):
        cut = slice(q * BLK, (q + 1) * BLK)
        hi = jnp.concatenate([x[0][:, cut] for x in dn_parts], axis=1)
        lo = jnp.concatenate([x[1][:, cut] for x in dn_parts], axis=1)
        r = dot(hi, weight(q))
        columns.append(r[:, :BLK] + r[:, BLK:] + dot(lo, weight(q)[:, :BLK]))
    total = jnp.concatenate(columns, axis=1)
    blocks = []
    for p in range(span // BLK):
        cut = slice(p * BLK, (p + 1) * BLK)
        block = lax.axis_index("up") * 16 + first + step * (span // BLK) + p
        w = jnp.concatenate(
            [signed(up_w, slots[t], signs_up[places[t], block].astype(F32)) for t in range(len(slots))], axis=1
        )
        r = dot(w, jnp.concatenate([x[0][cut] for x in up_parts], axis=0))
        blocks.append(
            r[:BLK] + r[BLK:] + dot(w[:BLK], jnp.concatenate([x[1][cut] for x in up_parts], axis=0))
        )
    return total + jnp.concatenate(blocks, axis=0)


def early_body(first, span, bits_up, signs_up, a0, a1, a2, mate, acc, up_w, rem_w, out):
    zero = lax.axis_index("dn") % 2 == 0
    slots = (jnp.where(zero, 7, 5), jnp.where(zero, 5, 7))
    ups = [a0[...], jnp.where(zero, a1[...], a2[...])]
    dns = [jnp.where(zero, a2[...], a1[...]), mate[...]]

    def weight(q):
        return jnp.concatenate([rem_w[q, :BLK], rem_w[q, 3 * BLK:]], axis=0)

    out[...] = acc[...] + remote(first, span, bits_up, signs_up, slots, ups, dns, up_w, weight)


def late_body(first, span, bits_up, signs_up, shift, b0, b1, b2, acc, own, up_w, rem_w,
               left, right, *rest):
    residual, updated, mark = rest[-3:]
    zero = lax.axis_index("dn") % 2 == 0
    ups = [jnp.where(zero, b1[...], b0[...])]
    dns = [jnp.where(zero, b0[...], b1[...]), b2[...]]

    def weight(q):
        return rem_w[q, BLK:3 * BLK]

    total = acc[...] + remote(first, span, bits_up, signs_up, (6,), ups, dns, up_w, weight)
    gap = lax.dot_general(left[...], right[...], (((0,), (0,)), ((), ())),
                          preferred_element_type=F32) - shift[0]
    c = own[...]
    res = total + gap * c
    residual[...] = res
    updated[...] = c - res / gap
    mark[...] = res[:8, :BLK]


def shards(
    coefficients,
    hopping_up,
    partner_bits_up,
    block_signs_up,
    hopping_down,
    partner_bits_down,
    block_signs_down,
    occupied_up,
    occupied_down,
    site_energy,
    repulsion,
    energy_shift,
):
    rows, width = coefficients.shape
    chunks = len(SIZES)
    starts = [sum(SIZES[:i]) * BLK for i in range(chunks)]
    vmem = pl.BlockSpec(memory_space=pltpu.VMEM)
    up_w, loc_w, rem_w, left, right = pl.pallas_call(
        prepare,
        out_shape=[
            jax.ShapeDtypeStruct((8, 2 * BLK, BLK), B16),
            jax.ShapeDtypeStruct((width, 2 * width), B16),
            jax.ShapeDtypeStruct((4, 4 * BLK, 2 * BLK), B16),
            jax.ShapeDtypeStruct((144, rows), B16),
            jax.ShapeDtypeStruct((144, width), B16),
        ],
        in_specs=[SMEM] * 5 + [vmem] * 4,
        scratch_shapes=[pltpu.VMEM((16, rows), F32), pltpu.VMEM((16, width), F32)],
        compiler_params=params(ROOM),
        cost_estimate=pl.CostEstimate(flops=0, bytes_accessed=4 << 20, transcendentals=0),
        name="prepare",
    )(partner_bits_up, partner_bits_down, block_signs_down, site_energy, repulsion,
      hopping_up, hopping_down, occupied_up, occupied_down)

    block = (4 * BLK, width)
    parts, pieces = [], [lax.slice_in_dim(coefficients, 0, SIZES[0] * BLK)]
    for h in range(2):
        own = [i for i in range(1, chunks) if starts[i] * 2 // rows == h]
        part, *more = pl.pallas_call(
            functools.partial(local_body, h, [starts[i] // BLK for i in own]),
            grid=(2,),
            out_shape=[jax.ShapeDtypeStruct((rows // 2, width), F32)]
            + [jax.ShapeDtypeStruct((SIZES[i] * BLK, width), F32) for i in own],
            in_specs=[
                SMEM,
                SMEM,
                pl.BlockSpec(block, lambda i, h=h: (2 * h + i, 0)),
                pl.BlockSpec(block, lambda i, h=h: ((2 * h + i) ^ 1, 0)),
                pl.BlockSpec(block, lambda i, h=h: ((2 * h + i) ^ 2, 0)),
                whole(up_w.shape),
                whole(loc_w.shape),
            ],
            out_specs=[pl.BlockSpec(block, lambda i: (i, 0))] + [whole((SIZES[i] * BLK, width)) for i in own],
            compiler_params=params(ROOM),
            cost_estimate=pl.CostEstimate(flops=6 << 30, bytes_accessed=12 << 20, transcendentals=0),
            name="local",
        )(partner_bits_up, block_signs_up, coefficients, coefficients, coefficients, up_w, loc_w)
        parts.append(part)
        pieces += more

    def finish(i, outs):
        span = 2 * BLK if (SIZES[i] | starts[i] // BLK) % 2 == 0 else BLK
        tile = (span, width)
        base = starts[i] // span
        here = pl.BlockSpec(tile, lambda s: (s, 0))
        there = pl.BlockSpec(tile, lambda s: (base + s, 0))
        h = starts[i] * 2 // rows
        below = h * rows // 2 // span
        half = pl.BlockSpec(tile, lambda s: (base - below + s, 0))
        arrived = [got[k, j, i] for k in "AB" for j in range(3)]
        operands = [partner_bits_up, block_signs_up, energy_shift.reshape(1), *arrived, got["mate"], got["acc", h], coefficients,
                    up_w, rem_w, left, right]
        tail = [*outs, got["mark"]] if outs else []
        body = final_body
        near = [here] * 6 + [there, half, there]
        if i in EARLY:
            sofar = pl.pallas_call(
                functools.partial(early_body, starts[i] // BLK, span),
                grid=(SIZES[i] * BLK // span,),
                out_shape=jax.ShapeDtypeStruct((SIZES[i] * BLK, width), F32),
                in_specs=[SMEM] * 2 + [here] * 3 + [there, half, whole(up_w.shape), whole(rem_w.shape)],
                out_specs=here,
                compiler_params=params(ROOM),
                cost_estimate=pl.CostEstimate(flops=2 << 30, bytes_accessed=8 << 20, transcendentals=0),
                name="early",
            )(*operands[:2], *arrived[:3], got["mate"], got["acc", h], up_w, rem_w)
            operands[3:11] = [*arrived[3:], sofar]
            body = late_body
            near = [here] * 4 + [there]
        return pl.pallas_call(
            functools.partial(body, starts[i] // BLK, span),
            grid=(SIZES[i] * BLK // span,),
            out_shape=[jax.ShapeDtypeStruct((rows, width), F32)] * 2 + [jax.ShapeDtypeStruct((8, BLK), F32)],
            in_specs=[SMEM] * 3 + near + [
                whole(up_w.shape),
                whole(rem_w.shape),
                pl.BlockSpec((144, span), lambda s: (0, base + s)),
                whole(right.shape),
            ] + [pl.BlockSpec(memory_space=pl.ANY)] * len(tail),
            out_specs=[there, there, whole((8, BLK))],
            input_output_aliases={len(operands) + k: k for k in range(len(outs))},
            compiler_params=params(ROOM),
            cost_estimate=pl.CostEstimate(flops=3 << 30, bytes_accessed=12 << 20, transcendentals=0),
            name="finish",
        )(*operands, *tail)

    order = [("A", j, 0) for j in range(3)]
    for i in range(chunks):
        for j in range(3):
            order.append(("B", j, i))
            if i + 1 < chunks:
                order.append(("A", j, i + 1))
    got, outs = {}, []
    got["mate"] = exchange(coefficients, (0, 1), (0, 1))
    got["acc", 0], got["acc", 1] = parts
    for n, (kind, j, i) in enumerate(order):
        source = pieces[i] if kind == "A" else got["A", j, i]
        waits = [("acc", 0), "mate"] if n == 3 else []
        if n >= GAP and order[n - GAP][:2] == ("B", 2):
            *outs, got["mark"] = finish(order[n - GAP][2], outs)
            waits = ["mark"]
        if waits:
            source, *held = lax.optimization_barrier((source, *[got[w] for w in waits]))
            got.update(zip(waits, held))
        if kind == "B":
            got["A", j, i] = source
        got[kind, j, i] = exchange(source, MASKS[kind][TURN[0][j]], MASKS[kind][TURN[1][j]])
    for n in range(len(order), len(order) + GAP):
        if order[n - GAP][:2] == ("B", 2):
            *outs, got["mark"] = finish(order[n - GAP][2], outs)
    return tuple(outs)


def solution(mesh):
    placed = (
        P("up", "dn"),
        P(),
        P(),
        P(),
        P(),
        P(),
        P(),
        P(None, "up"),
        P(None, "dn"),
        P(),
        P(),
        P(),
    )
    return jax.shard_map(
        shards,
        mesh=mesh,
        in_specs=placed,
        out_specs=(P("up", "dn"), P("up", "dn")),
        check_vma=False,
    )
```
